32 devices in a mesh: dp: 2 (over core), seq: 16 (over z, y, x).
Axes of the slice: x: 2, y: 2, z: 4, core: 2. Of those that a mesh axis runs over, the one named last changes fastest.
Arguments:
- inputs: bfloat16 [2, 16384, 2048], P('dp', 'seq'), may hold values from -45 to 45, as said below
- upstream: bfloat16 [2, 16384, 2048], P('dp', 'seq'), may hold values from -1 to 1
- right_blocks: bfloat16 [128, 128, 128], P('seq'), may hold values from -0.5 to 0.5
- left_blocks: bfloat16 [128, 128, 128], P('seq'), may hold values from -0.5 to 0.5
- gain: float32 [2048], replicated, may hold values from 0.1 to 1.9
- mid_scale: float32 [2048], replicated, may hold values from 0.5 to 2.5
Outputs:
- output: bfloat16 [2, 16384, 2048], P('dp', 'seq')
- input_gradient: bfloat16 [2, 16384, 2048], P('dp', 'seq')
- grad_right: float32 [128, 128, 128], P('seq')
- grad_left: float32 [128, 128, 128], P('seq')
- gain_gradient: float32 [2048], replicated
- grad_mid: float32 [2048], replicated
The draws below stay inside these ranges and needn't reach their ends.
Inputs may be any that keep to these rules, and one draw needn't show every extreme that they name: `inputs`: activations with independent scales per position and per channel.
All inputs are finite; a program needn't handle non-finite values.
Results may differ from the reference program's by a relative error of at most 0.0063.
Values may be sent and summed in bfloat16 or wider, within the bound.
No kernel may reach another device: no remote copies, remote signals or barrier semaphores. Data moves between devices by JAX's collectives and lax.ppermute only.
A program may use at most 128 MiB of HBM per device.

```python
import math
import jax
import jax.numpy as jnp
from jax import lax

D = 2048
BLK = 128
SEQ = 16384
BATCH = 2


def draw_inputs(key, part):
    key_base = jax.random.fold_in(key, 11)
    key_rows = jax.random.fold_in(key, 12)
    key_cols = jax.random.fold_in(key, 13)
    base = jnp.clip(jax.random.normal(key_base, (BATCH, SEQ, D), jnp.float32), -5.0, 5.0)
    rows = jnp.exp(jax.random.uniform(key_rows, (BATCH, SEQ, 1), jnp.float32, math.log(0.3), math.log(3.0)))
    cols = jnp.exp(jax.random.uniform(key_cols, (D,), jnp.float32, math.log(0.3), math.log(3.0)))
    return (base * rows * cols).astype(jnp.bfloat16)


def draw_upstream(key, part):
    key_base = jax.random.fold_in(key, 21)
    ramp = 1.0 + 2.0 * jnp.arange(SEQ, dtype=jnp.float32) / SEQ
    batch_ramp = 1.0 + jnp.arange(BATCH, dtype=jnp.float32) / BATCH
    scale = 0.03 * ramp[None, :, None] * batch_ramp[:, None, None]
    base = jnp.clip(jax.random.normal(key_base, (BATCH, SEQ, D), jnp.float32), -5.0, 5.0)
    return (base * scale).astype(jnp.bfloat16)


def levels(stream_key, extent, split, smallest, high):
    level, own = 1.0, jax.random.fold_in(stream_key, 6)
    for position, parts in split:
        draws = jnp.exp(jax.random.uniform(jax.random.fold_in(own, position), (parts,), jnp.float32, smallest / len(split), high / len(split)))
        level = level * jnp.repeat(draws, extent[position] // parts).reshape([-1 if axis == position else 1 for axis in range(len(extent))])
    return level


def scatter_about(key, extent, width, most, shards=(), held_as=jnp.bfloat16):
    level = levels(key, extent, shards, -0.22, 0.18) if shards else 1.0
    array = jax.random.normal(key, extent, jnp.float32) * width * level
    return jnp.minimum(jnp.maximum(array, -most), most).astype(held_as)


def setup_inputs(seed: int = 0) -> dict:
    key_of = jax.random.split(jax.random.key(seed), 7)
    return {
        "inputs": draw_inputs(jax.random.fold_in(key_of[6], 71), 0),
        "upstream": draw_upstream(jax.random.fold_in(key_of[6], 71), 0),
        "right_blocks": scatter_about(key_of[2], (BLK, BLK, BLK), BLK ** -0.5, 0.5, ((0, 16),)),
        "left_blocks": scatter_about(key_of[3], (BLK, BLK, BLK), BLK ** -0.5, 0.5, ((0, 16),)),
        "gain": jnp.clip(1.0 + 0.18 * jax.random.normal(key_of[4], (D,), jnp.float32), 0.1, 1.9),
        "mid_scale": jnp.clip(jax.random.uniform(key_of[5], (D,), jnp.float32, 0.5, 2.5), 0.5, 2.5),
    }


def one_sequence(pair, right_blocks, left_blocks, gain, mid_scale):
    inputs, upstream = pair
    input_float = inputs.astype(jnp.float32)
    inverse_norm = lax.rsqrt(lax.optimization_barrier(jnp.mean(input_float * input_float, axis=-1, keepdims=True)) + 1e-06)
    standardized_input = input_float * inverse_norm
    normalized_rows = (standardized_input * gain).astype(jnp.bfloat16)
    grid = normalized_rows.reshape(BLK, BLK, D).astype(jnp.float32)
    rights = right_blocks.astype(jnp.float32)
    lefts = left_blocks.astype(jnp.float32)
    first = jnp.einsum('aij,ajd->aid', rights, grid)
    sig = jax.nn.sigmoid(first * mid_scale)
    gated = (first * sig).astype(jnp.bfloat16).astype(jnp.float32)
    mixed = jnp.einsum('bij,jbd->ibd', lefts, gated).astype(jnp.bfloat16)
    output = (input_float + mixed.reshape(SEQ, D).astype(jnp.float32)).astype(jnp.bfloat16)
    upward = upstream.reshape(BLK, BLK, D).astype(jnp.float32)
    grad_left = jnp.einsum('ibd,jbd->bij', upward, gated)
    dgated = jnp.einsum('bij,ibd->jbd', lefts, upward).astype(jnp.bfloat16).astype(jnp.float32)
    slope = sig * (1.0 - sig)
    dfirst = (dgated * (sig + first * mid_scale * slope)).astype(jnp.bfloat16).astype(jnp.float32)
    grad_mid = lax.optimization_barrier(jnp.sum(dgated * first * first * slope, axis=(0, 1)))
    grad_right = jnp.einsum('aid,ajd->aij', dfirst, grid)
    normalized_gradient = jnp.einsum('aij,aid->ajd', rights, dfirst).reshape(SEQ, D)
    gain_gradient = lax.optimization_barrier(jnp.sum(normalized_gradient * standardized_input, axis=0))
    centered_gradient = normalized_gradient * gain
    input_gradient = upstream.astype(jnp.float32) + inverse_norm * (centered_gradient - standardized_input * lax.optimization_barrier(jnp.mean(centered_gradient * standardized_input, axis=-1, keepdims=True)))
    return (output, input_gradient.astype(jnp.bfloat16), grad_right, grad_left, gain_gradient, grad_mid)

def reference(inputs, upstream, right_blocks, left_blocks, gain, mid_scale):

    def step(pair):
        return one_sequence(pair, right_blocks, left_blocks, gain, mid_scale)
    output, input_gradient, grad_right, grad_left, gain_gradient, grad_mid = lax.map(step, (inputs, upstream))
    return (output, input_gradient, lax.optimization_barrier(jnp.sum(grad_right, axis=0)), lax.optimization_barrier(jnp.sum(grad_left, axis=0)), lax.optimization_barrier(jnp.sum(gain_gradient, axis=0)), lax.optimization_barrier(jnp.sum(grad_mid, axis=0)))
```

```python
import jax
import jax.numpy as jnp
from jax import lax
from jax.sharding import PartitionSpec as P


def to_offsets(rows):
    return lax.all_to_all(rows, "seq", 1, 0, tiled=True)


def to_blocks(rows):
    return lax.all_to_all(rows, "seq", 0, 1, tiled=True)


def body(inputs, upstream, right_blocks, left_blocks, gain, mid_scale):
    count = lax.axis_size("seq")
    rows = inputs.shape[1]
    width = inputs.shape[2]
    order = right_blocks.shape[1]
    local = order // count
    f32 = jnp.float32
    bf16 = jnp.bfloat16
    upward = to_offsets(upstream[0].reshape(local, order, width))
    input_float = inputs[0].astype(f32)
    inverse_norm = lax.rsqrt(jnp.mean(input_float * input_float, axis=-1, keepdims=True) + 1e-06)
    standardized_input = input_float * inverse_norm
    normalized_rows = (standardized_input * gain).astype(bf16)
    grid = normalized_rows.reshape(local, order, width)
    first = jnp.einsum("aij,ajd->aid", right_blocks, grid, preferred_element_type=f32)
    sig = jax.nn.sigmoid(first * mid_scale)
    gated = (first * sig).astype(bf16)
    arrived = to_offsets(gated)
    returned = jnp.einsum("bij,ibd->jbd", left_blocks, upward, preferred_element_type=f32).astype(bf16)
    dgated = to_blocks(returned).astype(f32)
    mixed = jnp.einsum("bij,jbd->ibd", left_blocks, arrived, preferred_element_type=f32).astype(bf16)
    back = to_blocks(mixed).reshape(rows, width)
    grad_left = jnp.einsum("ibd,jbd->bij", upward, arrived, preferred_element_type=f32)
    output = (input_float + back.astype(f32)).astype(bf16)
    slope = sig * (1.0 - sig)
    dfirst = (dgated * (sig + first * mid_scale * slope)).astype(bf16)
    mid_part = jnp.sum(dgated * first * first * slope, axis=(0, 1))
    grad_right = jnp.einsum("aid,ajd->aij", dfirst, grid, preferred_element_type=f32)
    normalized_gradient = jnp.einsum(
        "aij,aid->ajd", right_blocks, dfirst, preferred_element_type=f32
    ).reshape(rows, width)
    gain_slice = jnp.sum(normalized_gradient * standardized_input, axis=0)
    centered_gradient = normalized_gradient * gain
    input_gradient = upstream[0].astype(f32) + inverse_norm * (
        centered_gradient
        - standardized_input
        * jnp.mean(centered_gradient * standardized_input, axis=-1, keepdims=True)
    )
    input_gradient = input_gradient.astype(bf16)
    grad_left = lax.psum(grad_left, "dp")
    grad_right = lax.psum(grad_right, "dp")
    gain_gradient, grad_mid = lax.psum((gain_slice, mid_part), ("dp", "seq"))
    return (
        output.reshape(1, rows, width),
        input_gradient.reshape(1, rows, width),
        grad_right,
        grad_left,
        gain_gradient,
        grad_mid,
    )


def solution(mesh):
    in_specs = (
        P("dp", "seq", None),
        P("dp", "seq", None),
        P("seq", None, None),
        P("seq", None, None),
        P(),
        P(),
    )
    out_specs = (
        P("dp", "seq", None),
        P("dp", "seq", None),
        P("seq", None, None),
        P("seq", None, None),
        P(),
        P(),
    )
    return jax.shard_map(body, mesh=mesh, in_specs=in_specs, out_specs=out_specs, check_vma=False)
```

```python
import jax
import jax.numpy as jnp
from jax import lax
from jax.sharding import PartitionSpec as P


def to_offsets(rows):
    count = lax.axis_size("seq")
    height, span, width = rows.shape
    parts = rows.reshape(height, count, span // count, width).swapaxes(0, 1)
    parts = lax.all_to_all(parts, "seq", 0, 0, tiled=True)
    return parts.reshape(count * height, span // count, width)


def to_blocks(rows):
    count = lax.axis_size("seq")
    span, height, width = rows.shape
    parts = rows.reshape(count, span // count, height, width)
    parts = lax.all_to_all(parts, "seq", 0, 0, tiled=True)
    return parts.swapaxes(0, 1).reshape(span // count, count * height, width)


def body(inputs, upstream, right_blocks, left_blocks, gain, mid_scale):
    count = lax.axis_size("seq")
    rows = inputs.shape[1]
    width = inputs.shape[2]
    order = right_blocks.shape[1]
    local = order // count
    f32 = jnp.float32
    bf16 = jnp.bfloat16
    upward = to_offsets(upstream[0].reshape(local, order, width))
    input_float = inputs[0].astype(f32)
    inverse_norm = lax.rsqrt(jnp.mean(input_float * input_float, axis=-1, keepdims=True) + 1e-06)
    standardized_input = input_float * inverse_norm
    normalized_rows = (standardized_input * gain).astype(bf16)
    grid = normalized_rows.reshape(local, order, width)
    first = jnp.einsum("aij,ajd->aid", right_blocks, grid, preferred_element_type=f32)
    sig = jax.nn.sigmoid(first * mid_scale)
    gated = (first * sig).astype(bf16)
    gated, upward = lax.optimization_barrier((gated, upward))
    arrived = to_offsets(gated)
    returned = jnp.einsum("bij,ibd->jbd", left_blocks, upward, preferred_element_type=f32).astype(bf16)
    arrived, returned = lax.optimization_barrier((arrived, returned))
    dgated = to_blocks(returned)
    mixed = jnp.einsum("bij,jbd->ibd", left_blocks, arrived, preferred_element_type=f32).astype(bf16)
    grad_left = jnp.einsum("ibd,jbd->bij", upward, arrived, preferred_element_type=f32)
    mixed, dgated, grad_left = lax.optimization_barrier((mixed, dgated, grad_left))
    back = to_blocks(mixed).reshape(rows, width)
    output = (input_float + back.astype(f32)).astype(bf16)
    dgated = dgated.astype(f32)
    slope = sig * (1.0 - sig)
    dfirst = (dgated * (sig + first * mid_scale * slope)).astype(bf16)
    mid_part = jnp.sum(dgated * first * first * slope, axis=(0, 1))
    grad_right = jnp.einsum("aid,ajd->aij", dfirst, grid, preferred_element_type=f32)
    normalized_gradient = jnp.einsum(
        "aij,aid->ajd", right_blocks, dfirst, preferred_element_type=f32
    ).reshape(rows, width)
    gain_slice = jnp.sum(normalized_gradient * standardized_input, axis=0)
    centered_gradient = normalized_gradient * gain
    input_gradient = upstream[0].astype(f32) + inverse_norm * (
        centered_gradient
        - standardized_input
        * jnp.mean(centered_gradient * standardized_input, axis=-1, keepdims=True)
    )
    input_gradient = input_gradient.astype(bf16)
    grad_left = lax.psum(grad_left, "dp")
    grad_right = lax.psum(grad_right, "dp")
    vectors = lax.all_gather(jnp.stack((gain_slice, mid_part)), ("dp", "seq"))
    gain_gradient, grad_mid = jnp.sum(vectors, axis=0)
    return (
        output.reshape(1, rows, width),
        input_gradient.reshape(1, rows, width),
        grad_right,
        grad_left,
        gain_gradient,
        grad_mid,
    )


def solution(mesh):
    in_specs = (
        P("dp", "seq", None),
        P("dp", "seq", None),
        P("seq", None, None),
        P("seq", None, None),
        P(),
        P(),
    )
    out_specs = (
        P("dp", "seq", None),
        P("dp", "seq", None),
        P("seq", None, None),
        P("seq", None, None),
        P(),
        P(),
    )
    return jax.shard_map(body, mesh=mesh, in_specs=in_specs, out_specs=out_specs, check_vma=False)
```

```python
import jax
import jax.numpy as jnp
from jax import lax
from jax.sharding import PartitionSpec as P


def from_partner(block, axis, distance):
    if distance == 0:
        return block
    count = lax.axis_size(axis)
    return lax.ppermute(block, axis, [(i, i ^ distance) for i in range(count)])


def tree_sum(terms):
    while len(terms) > 1:
        terms = [terms[i] + terms[i + 1] for i in range(0, len(terms), 2)]
    return terms[0]


def sum_over(value, axis, low, high):
    return tree_sum([from_partner(value, axis, k << low) for k in range(1 << high - low)])


def after(value, other):
    return lax.optimization_barrier((value, other))[0]


def body(inputs, upstream, right_blocks, left_blocks, gain, mid_scale):
    count = lax.axis_size("seq")
    levels = count.bit_length() - 1
    low = levels // 2
    near = 1 << low
    far = count // near
    dp_levels = lax.axis_size("dp").bit_length() - 1
    device = lax.axis_index("seq")
    device_near = device & near - 1
    device_far = device >> low
    rows = inputs.shape[1]
    width = inputs.shape[2]
    order = right_blocks.shape[1]
    local = order // count
    f32 = jnp.float32
    bf16 = jnp.bfloat16

    place = lax.broadcasted_iota(jnp.int32, (order, order), 0)
    swap = (place ^ device * local) == lax.broadcasted_iota(jnp.int32, (order, order), 1)
    swap_half = swap.astype(bf16)
    swap_full = swap.astype(f32)
    rights = jnp.einsum("ki,aij->akj", swap_half, right_blocks)
    lefts = jnp.einsum("aij,jl->ail", jnp.einsum("ki,aij->akj", swap_half, left_blocks), swap_half)

    up_view = upstream[0].reshape(local, far, near, local, width)
    up_parts = [lax.dynamic_index_in_dim(up_view, device_far ^ k, 1, keepdims=False) for k in range(far)]
    up_far = [from_partner(up_parts[k], "seq", k << low) for k in range(far)]
    inputs = after(inputs, up_parts)
    input_float = inputs[0].astype(f32)
    inverse_norm = lax.rsqrt(jnp.mean(input_float * input_float, axis=-1, keepdims=True) + 1e-06)
    standardized_input = input_float * inverse_norm
    normalized_rows = (standardized_input * gain).astype(bf16)
    grid = normalized_rows.reshape(local, order, width)
    first = jnp.einsum("aij,ajd->aid", rights, grid, preferred_element_type=f32)
    sig = jax.nn.sigmoid(first * mid_scale)
    gated = (first * sig).astype(bf16)

    gated_view = gated.reshape(local, far, near, local, width)
    gated_near = [from_partner(gated_view[:, :, k], "seq", k) for k in range(near)]
    gated_near = [jnp.stack([t[:, k] for t in gated_near]) for k in range(far)]
    gated_far = [from_partner(gated_near[k], "seq", k << low) for k in range(far)]
    up_far = after(up_far, gated_near)
    up_near = [
        from_partner(
            jnp.stack([lax.dynamic_index_in_dim(t, device_near ^ k, 1, keepdims=False) for t in up_far]), "seq", k
        )
        for k in range(near)
    ]
    upward = jnp.stack(up_near, axis=1).reshape(order, local, width)
    returned = jnp.einsum("bij,ibd->jbd", lefts, upward, preferred_element_type=f32).astype(bf16)
    returned = returned.reshape(far, near, local, local, width)
    back_far = [from_partner(returned[k], "seq", k << low) for k in range(far)]
    gated_far = after(gated_far, returned)
    arrived = jnp.stack(gated_far).reshape(order, local, width)
    mixed = jnp.einsum("bij,jbd->ibd", lefts, arrived, preferred_element_type=f32).astype(bf16)
    mixed = mixed.reshape(far, near, local, local, width)
    mixed_near = jnp.zeros((far, near, local, local, width), bf16)
    for k in range(near):
        mixed_near = lax.dynamic_update_index_in_dim(
            mixed_near, from_partner(mixed[:, k], "seq", k), device_near ^ k, 1
        )
    back_far = after(back_far, mixed_near)
    back_near = [from_partner(jnp.stack([t[k] for t in back_far]), "seq", k) for k in range(near)]
    dgated = jnp.stack(back_near, axis=1).transpose(2, 0, 1, 3, 4).reshape(local, order, width).astype(f32)

    upward, arrived = after((upward, arrived), mixed)
    grad_left = jnp.einsum("ibd,jbd->bij", upward, arrived, preferred_element_type=f32)
    grad_left = sum_over(grad_left, "dp", 0, dp_levels)
    grad_left = jnp.einsum("ki,aij->akj", swap_full, grad_left, precision=lax.Precision.HIGHEST)
    grad_left = jnp.einsum("aij,jl->ail", grad_left, swap_full, precision=lax.Precision.HIGHEST)

    slope = sig * (1.0 - sig)
    dfirst = (dgated * (sig + first * mid_scale * slope)).astype(bf16)
    mid_part = jnp.sum(dgated * first * first * slope, axis=(0, 1))
    grad_right = jnp.einsum("aid,ajd->aij", dfirst, grid, preferred_element_type=f32)
    grad_right = sum_over(grad_right, "dp", 0, dp_levels)
    grad_right = jnp.einsum("ki,aij->akj", swap_full, grad_right, precision=lax.Precision.HIGHEST)
    normalized_gradient = jnp.einsum(
        "aij,aid->ajd", rights, dfirst, preferred_element_type=f32
    ).reshape(rows, width)
    gain_slice = jnp.sum(normalized_gradient * standardized_input, axis=0)
    centered_gradient = normalized_gradient * gain
    input_gradient = upstream[0].astype(f32) + inverse_norm * (
        centered_gradient
        - standardized_input
        * jnp.mean(centered_gradient * standardized_input, axis=-1, keepdims=True)
    )
    input_gradient = input_gradient.astype(bf16)
    vectors = jnp.stack((gain_slice, mid_part))
    vectors = sum_over(vectors, "dp", 0, dp_levels)
    vectors = sum_over(vectors, "seq", 0, low)
    gain_gradient, grad_mid = sum_over(vectors, "seq", low, levels)
    output = jnp.zeros((local, far, near, local, width), bf16)
    input_view = inputs[0].reshape(local, far, near, local, width)
    mixed_far = [from_partner(mixed_near[k], "seq", k << low) for k in range(far)]
    mixed_far = after(mixed_far, (input_gradient, grad_right))
    for k in range(far):
        place = device_far ^ k
        part = mixed_far[k].swapaxes(0, 1)
        residual = lax.dynamic_index_in_dim(input_view, place, 1, keepdims=False).astype(f32)
        output = lax.dynamic_update_index_in_dim(output, (residual + part.astype(f32)).astype(bf16), place, 1)
    return (
        output.reshape(1, rows, width),
        input_gradient.reshape(1, rows, width),
        grad_right,
        grad_left,
        gain_gradient,
        grad_mid,
    )


def solution(mesh):
    in_specs = (
        P("dp", "seq", None),
        P("dp", "seq", None),
        P("seq", None, None),
        P("seq", None, None),
        P(),
        P(),
    )
    out_specs = (
        P("dp", "seq", None),
        P("dp", "seq", None),
        P("seq", None, None),
        P("seq", None, None),
        P(),
        P(),
    )
    return jax.shard_map(body, mesh=mesh, in_specs=in_specs, out_specs=out_specs, check_vma=False)
```

```python
import jax
import jax.numpy as jnp
from jax import lax
from jax.sharding import PartitionSpec as P


def from_partner(block, axis, distance):
    if distance == 0:
        return block
    count = lax.axis_size(axis)
    return lax.ppermute(block, axis, [(i, i ^ distance) for i in range(count)])


def tree_sum(terms):
    while len(terms) > 1:
        terms = [terms[i] + terms[i + 1] for i in range(0, len(terms), 2)]
    return terms[0]


def sum_over(value, axis, low, high):
    return tree_sum([from_partner(value, axis, k << low) for k in range(1 << high - low)])


def body(inputs, upstream, right_blocks, left_blocks, gain, mid_scale):
    count = lax.axis_size("seq")
    levels = count.bit_length() - 1
    low = levels // 2
    near = 1 << low
    far = count // near
    dp_levels = lax.axis_size("dp").bit_length() - 1
    device = lax.axis_index("seq")
    device_near = device & near - 1
    device_far = device >> low
    rows = inputs.shape[1]
    width = inputs.shape[2]
    order = right_blocks.shape[1]
    local = order // count
    f32 = jnp.float32
    bf16 = jnp.bfloat16

    place = lax.broadcasted_iota(jnp.int32, (order, order), 0)
    swap = (place ^ device * local) == lax.broadcasted_iota(jnp.int32, (order, order), 1)
    swap_half = swap.astype(bf16)
    swap_full = swap.astype(f32)
    rights = jnp.einsum("ki,aij->akj", swap_half, right_blocks)
    lefts = jnp.einsum("aij,jl->ail", jnp.einsum("ki,aij->akj", swap_half, left_blocks), swap_half)

    up_view = upstream[0].reshape(local, far, near, local, width)
    up_parts = [lax.dynamic_index_in_dim(up_view, device_far ^ k, 1, keepdims=False) for k in range(far)]
    up_far = [from_partner(up_parts[k], "seq", k << low) for k in range(1, far)]
    inputs, up_here = lax.optimization_barrier((inputs, up_parts[0]))
    input_float = inputs[0].astype(f32)
    inverse_norm = lax.rsqrt(jnp.mean(input_float * input_float, axis=-1, keepdims=True) + 1e-06)
    standardized_input = input_float * inverse_norm
    normalized_rows = (standardized_input * gain).astype(bf16)
    grid = normalized_rows.reshape(local, order, width)
    first = jnp.einsum("aij,ajd->aid", rights, grid, preferred_element_type=f32)
    sig = jax.nn.sigmoid(first * mid_scale)
    gated = (first * sig).astype(bf16)

    gated_view = gated.reshape(local, far, near, local, width)
    gated_near = [from_partner(gated_view[:, :, k], "seq", k) for k in range(near)]
    gated_near = [jnp.stack([t[:, k] for t in gated_near]) for k in range(far)]
    gated_far = [from_partner(gated_near[k], "seq", k << low) for k in range(1, far)]
    up_far, gated_here = lax.optimization_barrier((up_far, gated_near[0]))
    up_far = [up_here] + up_far
    up_near = [
        from_partner(
            jnp.stack([lax.dynamic_index_in_dim(t, device_near ^ k, 1, keepdims=False) for t in up_far]), "seq", k
        )
        for k in range(near)
    ]
    upward = jnp.stack(up_near, axis=1).reshape(order, local, width)
    returned = jnp.einsum("bij,ibd->jbd", lefts, upward, preferred_element_type=f32).astype(bf16)
    returned = returned.reshape(far, near, local, local, width)
    back_far = [from_partner(returned[k], "seq", k << low) for k in range(1, far)]
    gated_far, returned_here = lax.optimization_barrier((gated_far, returned[0]))
    arrived = jnp.stack([gated_here] + gated_far).reshape(order, local, width)
    mixed = jnp.einsum("bij,jbd->ibd", lefts, arrived, preferred_element_type=f32).astype(bf16)
    mixed = mixed.reshape(far, near, local, local, width)
    mixed_here = mixed[:, 0]
    mixed_sent = [from_partner(mixed[:, k], "seq", k) for k in range(1, near)]
    upward, arrived, mixed_here = lax.optimization_barrier((upward, arrived, mixed_here))
    mixed_near = jnp.zeros((far, near, local, local, width), bf16)
    for k, part in enumerate([mixed_here] + mixed_sent):
        mixed_near = lax.dynamic_update_index_in_dim(mixed_near, part, device_near ^ k, 1)
    mixed_far = [from_partner(mixed_near[k], "seq", k << low) for k in range(1, far)]
    back_far, mixed_here = lax.optimization_barrier((back_far, mixed_near[0]))
    back_far = [returned_here] + back_far
    back_near = [from_partner(jnp.stack([t[k] for t in back_far]), "seq", k) for k in range(near)]
    dgated = jnp.stack(back_near, axis=1).transpose(2, 0, 1, 3, 4).reshape(local, order, width).astype(f32)

    grad_left = jnp.einsum("ibd,jbd->bij", upward, arrived, preferred_element_type=f32)
    grad_left = sum_over(grad_left, "dp", 0, dp_levels)
    grad_left = jnp.einsum("ki,aij->akj", swap_full, grad_left, precision=lax.Precision.HIGHEST)
    grad_left = jnp.einsum("aij,jl->ail", grad_left, swap_full, precision=lax.Precision.HIGHEST)

    slope = sig * (1.0 - sig)
    dfirst = (dgated * (sig + first * mid_scale * slope)).astype(bf16)
    mid_part = jnp.sum(dgated * first * first * slope, axis=(0, 1))
    grad_right = jnp.einsum("aid,ajd->aij", dfirst, grid, preferred_element_type=f32)
    grad_right = sum_over(grad_right, "dp", 0, dp_levels)
    grad_right = jnp.einsum("ki,aij->akj", swap_full, grad_right, precision=lax.Precision.HIGHEST)
    normalized_gradient = jnp.einsum(
        "aij,aid->ajd", rights, dfirst, preferred_element_type=f32
    ).reshape(rows, width)
    gain_slice = jnp.sum(normalized_gradient * standardized_input, axis=0)
    centered_gradient = normalized_gradient * gain
    input_gradient = upstream[0].astype(f32) + inverse_norm * (
        centered_gradient
        - standardized_input
        * jnp.mean(centered_gradient * standardized_input, axis=-1, keepdims=True)
    )
    input_gradient = input_gradient.astype(bf16)
    vectors = jnp.stack((gain_slice, mid_part))
    vectors = sum_over(vectors, "dp", 0, dp_levels)
    vectors = sum_over(vectors, "seq", 0, low)
    gain_gradient, grad_mid = sum_over(vectors, "seq", low, levels)
    output = jnp.zeros((local, far, near, local, width), bf16)
    input_view = inputs[0].reshape(local, far, near, local, width)
    mixed_far, input_gradient = lax.optimization_barrier((mixed_far, input_gradient))
    mixed_far = [mixed_here] + mixed_far
    for k in range(far):
        place = device_far ^ k
        part = mixed_far[k].swapaxes(0, 1)
        residual = lax.dynamic_index_in_dim(input_view, place, 1, keepdims=False).astype(f32)
        output = lax.dynamic_update_index_in_dim(output, (residual + part.astype(f32)).astype(bf16), place, 1)
    return (
        output.reshape(1, rows, width),
        input_gradient.reshape(1, rows, width),
        grad_right,
        grad_left,
        gain_gradient,
        grad_mid,
    )


def solution(mesh):
    in_specs = (
        P("dp", "seq", None),
        P("dp", "seq", None),
        P("seq", None, None),
        P("seq", None, None),
        P(),
        P(),
    )
    out_specs = (
        P("dp", "seq", None),
        P("dp", "seq", None),
        P("seq", None, None),
        P("seq", None, None),
        P(),
        P(),
    )
    return jax.shard_map(body, mesh=mesh, in_specs=in_specs, out_specs=out_specs, check_vma=False)
```

```python
import jax
import jax.numpy as jnp
from jax import lax
from jax.sharding import PartitionSpec as P


def from_partner(block, axis, distance):
    if distance == 0:
        return block
    count = lax.axis_size(axis)
    return lax.ppermute(block, axis, [(i, i ^ distance) for i in range(count)])


def tree_sum(terms):
    while len(terms) > 1:
        terms = [terms[i] + terms[i + 1] for i in range(0, len(terms), 2)]
    return terms[0]


def sum_over(value, axis, low, high):
    return tree_sum([from_partner(value, axis, k << low) for k in range(1 << high - low)])


def body(inputs, upstream, right_blocks, left_blocks, gain, mid_scale):
    count = lax.axis_size("seq")
    levels = count.bit_length() - 1
    low = levels // 2
    near = 1 << low
    far = count // near
    dp_levels = lax.axis_size("dp").bit_length() - 1
    device = lax.axis_index("seq")
    device_near = device & near - 1
    device_far = device >> low
    rows = inputs.shape[1]
    width = inputs.shape[2]
    order = right_blocks.shape[1]
    local = order // count
    f32 = jnp.float32
    bf16 = jnp.bfloat16

    place = lax.broadcasted_iota(jnp.int32, (order, order), 0)
    swap = (place ^ device * local) == lax.broadcasted_iota(jnp.int32, (order, order), 1)
    swap_half = swap.astype(bf16)
    swap_full = swap.astype(f32)
    rights = jnp.einsum("ki,aij->akj", swap_half, right_blocks)
    lefts = jnp.einsum("aij,jl->ail", jnp.einsum("ki,aij->akj", swap_half, left_blocks), swap_half)

    up_view = upstream[0].reshape(local, far, near, local, width)
    up_parts = [lax.dynamic_index_in_dim(up_view, device_far ^ k, 1, keepdims=False) for k in range(far)]
    up_far = [from_partner(up_parts[k], "seq", k << low) for k in range(1, far)]
    inputs, up_here = lax.optimization_barrier((inputs, up_parts[0]))
    input_float = inputs[0].astype(f32)
    inverse_norm = lax.rsqrt(jnp.mean(input_float * input_float, axis=-1, keepdims=True) + 1e-06)
    standardized_input = input_float * inverse_norm
    normalized_rows = (standardized_input * gain).astype(bf16)
    grid = normalized_rows.reshape(local, order, width)
    first = jnp.einsum("aij,ajd->aid", rights, grid, preferred_element_type=f32)
    sig = jax.nn.sigmoid(first * mid_scale)
    gated = (first * sig).astype(bf16)

    gated_view = gated.reshape(local, far, near, local, width)
    gated_near = [from_partner(gated_view[:, :, k], "seq", k) for k in range(near)]
    gated_near = [jnp.stack([t[:, k] for t in gated_near]) for k in range(far)]
    up_far, gated_near = lax.optimization_barrier((up_far, gated_near))
    up_far = [up_here] + up_far
    gated_here = gated_near[0]
    gated_far = [from_partner(gated_near[k], "seq", k << low) for k in range(1, far)]
    up_near = [
        from_partner(
            jnp.stack([lax.dynamic_index_in_dim(t, device_near ^ k, 1, keepdims=False) for t in up_far]), "seq", k
        )
        for k in range(near)
    ]
    upward = jnp.stack(up_near, axis=1).reshape(order, local, width)
    returned = jnp.einsum("bij,ibd->jbd", lefts, upward, preferred_element_type=f32).astype(bf16)
    returned = returned.reshape(far, near, local, local, width)
    gated_far, returned = lax.optimization_barrier((gated_far, returned))
    returned_here = returned[0]
    back_far = [from_partner(returned[k], "seq", k << low) for k in range(1, far)]
    arrived = jnp.stack([gated_here] + gated_far).reshape(order, local, width)
    mixed = jnp.einsum("bij,jbd->ibd", lefts, arrived, preferred_element_type=f32).astype(bf16)
    mixed = mixed.reshape(far, near, local, local, width)
    mixed_here = mixed[:, 0]
    mixed_sent = [from_partner(mixed[:, k], "seq", k) for k in range(1, near)]
    upward, arrived, mixed_here = lax.optimization_barrier((upward, arrived, mixed_here))
    mixed_near = jnp.zeros((far, near, local, local, width), bf16)
    for k, part in enumerate([mixed_here] + mixed_sent):
        mixed_near = lax.dynamic_update_index_in_dim(mixed_near, part, device_near ^ k, 1)
    back_far, mixed_near = lax.optimization_barrier((back_far, mixed_near))
    back_far = [returned_here] + back_far
    mixed_here = mixed_near[0]
    mixed_far = [from_partner(mixed_near[k], "seq", k << low) for k in range(1, far)]
    back_near = [from_partner(jnp.stack([t[k] for t in back_far]), "seq", k) for k in range(near)]
    dgated = jnp.stack(back_near, axis=1).transpose(2, 0, 1, 3, 4).reshape(local, order, width).astype(f32)

    grad_left = jnp.einsum("ibd,jbd->bij", upward, arrived, preferred_element_type=f32)
    grad_left = sum_over(grad_left, "dp", 0, dp_levels)
    grad_left = jnp.einsum("ki,aij->akj", swap_full, grad_left, precision=lax.Precision.HIGHEST)
    grad_left = jnp.einsum("aij,jl->ail", grad_left, swap_full, precision=lax.Precision.HIGHEST)

    slope = sig * (1.0 - sig)
    dfirst = (dgated * (sig + first * mid_scale * slope)).astype(bf16)
    mid_part = jnp.sum(dgated * first * first * slope, axis=(0, 1))
    grad_right = jnp.einsum("aid,ajd->aij", dfirst, grid, preferred_element_type=f32)
    grad_right = sum_over(grad_right, "dp", 0, dp_levels)
    grad_right = jnp.einsum("ki,aij->akj", swap_full, grad_right, precision=lax.Precision.HIGHEST)
    normalized_gradient = jnp.einsum(
        "aij,aid->ajd", rights, dfirst, preferred_element_type=f32
    ).reshape(rows, width)
    gain_slice = jnp.sum(normalized_gradient * standardized_input, axis=0)
    centered_gradient = normalized_gradient * gain
    input_gradient = upstream[0].astype(f32) + inverse_norm * (
        centered_gradient
        - standardized_input
        * jnp.mean(centered_gradient * standardized_input, axis=-1, keepdims=True)
    )
    input_gradient = input_gradient.astype(bf16)
    vectors = jnp.stack((gain_slice, mid_part))
    vectors = sum_over(vectors, "dp", 0, dp_levels)
    vectors = sum_over(vectors, "seq", 0, low)
    gain_gradient, grad_mid = sum_over(vectors, "seq", low, levels)
    output = jnp.zeros((local, far, near, local, width), bf16)
    input_view = inputs[0].reshape(local, far, near, local, width)
    mixed_far, input_gradient, gain_gradient, grad_mid = lax.optimization_barrier(
        (mixed_far, input_gradient, gain_gradient, grad_mid)
    )
    mixed_far = [mixed_here] + mixed_far
    for k in range(far):
        place = device_far ^ k
        part = mixed_far[k].swapaxes(0, 1)
        residual = lax.dynamic_index_in_dim(input_view, place, 1, keepdims=False).astype(f32)
        output = lax.dynamic_update_index_in_dim(output, (residual + part.astype(f32)).astype(bf16), place, 1)
    return (
        output.reshape(1, rows, width),
        input_gradient.reshape(1, rows, width),
        grad_right,
        grad_left,
        gain_gradient,
        grad_mid,
    )


def solution(mesh):
    in_specs = (
        P("dp", "seq", None),
        P("dp", "seq", None),
        P("seq", None, None),
        P("seq", None, None),
        P(),
        P(),
    )
    out_specs = (
        P("dp", "seq", None),
        P("dp", "seq", None),
        P("seq", None, None),
        P("seq", None, None),
        P(),
        P(),
    )
    return jax.shard_map(body, mesh=mesh, in_specs=in_specs, out_specs=out_specs, check_vma=False)
```

```python
import jax
import jax.numpy as jnp
from jax import lax
from jax.sharding import PartitionSpec as P


def from_partner(block, axis, distance):
    if distance == 0:
        return block
    count = lax.axis_size(axis)
    return lax.ppermute(block, axis, [(i, i ^ distance) for i in range(count)])


def tree_sum(terms):
    while len(terms) > 1:
        terms = [terms[i] + terms[i + 1] for i in range(0, len(terms), 2)]
    return terms[0]


def sum_over(value, axis, low, high):
    return tree_sum([from_partner(value, axis, k << low) for k in range(1 << high - low)])


def body(inputs, upstream, right_blocks, left_blocks, gain, mid_scale):
    count = lax.axis_size("seq")
    levels = count.bit_length() - 1
    low = levels // 2
    near = 1 << low
    far = count // near
    dp_levels = lax.axis_size("dp").bit_length() - 1
    device = lax.axis_index("seq")
    device_near = device & near - 1
    device_far = device >> low
    rows = inputs.shape[1]
    width = inputs.shape[2]
    order = right_blocks.shape[1]
    local = order // count
    f32 = jnp.float32
    bf16 = jnp.bfloat16

    place = lax.broadcasted_iota(jnp.int32, (order, order), 0)
    swap = (place ^ device * local) == lax.broadcasted_iota(jnp.int32, (order, order), 1)
    swap_half = swap.astype(bf16)
    swap_full = swap.astype(f32)
    rights = jnp.einsum("ki,aij->akj", swap_half, right_blocks)
    lefts = jnp.einsum("aij,jl->ail", jnp.einsum("ki,aij->akj", swap_half, left_blocks), swap_half)

    half = far // 2
    rest = [k for k in range(1, far) if k != half]

    up_view = upstream[0].reshape(local, far, near, local, width)
    up_parts = [lax.dynamic_index_in_dim(up_view, device_far ^ k, 1, keepdims=False) for k in range(far)]
    up_far = [from_partner(up_parts[k], "seq", k << low) for k in range(far)]
    inputs, up_far[0] = lax.optimization_barrier((inputs, up_far[0]))
    input_float = inputs[0].astype(f32)
    inverse_norm = lax.rsqrt(jnp.mean(input_float * input_float, axis=-1, keepdims=True) + 1e-06)
    standardized_input = input_float * inverse_norm
    normalized_rows = (standardized_input * gain).astype(bf16)
    grid = normalized_rows.reshape(local, order, width)
    first = jnp.einsum("aij,ajd->aid", rights, grid, preferred_element_type=f32)
    sig = jax.nn.sigmoid(first * mid_scale)
    gated = (first * sig).astype(bf16)

    gated_view = gated.reshape(local, far, near, local, width)
    gated_near = [from_partner(gated_view[:, :, k], "seq", k) for k in range(near)]

    def sent_near(part):
        return [lax.dynamic_index_in_dim(part, device_near ^ k, 1, keepdims=False) for k in range(near)]

    up_half = sent_near(up_far[half])
    up_half, gated_near = lax.optimization_barrier((up_half, gated_near))
    gated_sent = [jnp.stack([t[:, k] for t in gated_near]) for k in range(far)]
    up_rest, gated_rest = lax.optimization_barrier(([up_far[k] for k in rest], [gated_sent[k] for k in rest]))
    for k, up_part, gated_part in zip(rest, up_rest, gated_rest):
        up_far[k], gated_sent[k] = up_part, gated_part
    gated_far = [from_partner(gated_sent[k], "seq", k << low) for k in range(far)]
    up_sent = [up_half if k == half else sent_near(up_far[k]) for k in range(far)]
    up_near = [from_partner(jnp.stack([t[k] for t in up_sent]), "seq", k) for k in range(near)]

    gated_pair = jnp.stack([gated_far[0], gated_far[half]])
    gated_pair, up_near = lax.optimization_barrier((gated_pair, up_near))
    gated_far[0], gated_far[half] = gated_pair[0], gated_pair[1]
    upward = jnp.stack(up_near, axis=1).reshape(order, local, width)
    returned = jnp.einsum("bij,ibd->jbd", lefts, upward, preferred_element_type=f32).astype(bf16)
    returned = list(returned.reshape(far, near, local, local, width))
    gated_rest, returned_rest = lax.optimization_barrier(
        ([gated_far[k] for k in rest], [returned[k] for k in rest])
    )
    for k, gated_part, returned_part in zip(rest, gated_rest, returned_rest):
        gated_far[k], returned[k] = gated_part, returned_part
    back_far = [from_partner(returned[k], "seq", k << low) for k in range(far)]

    arrived = jnp.stack(gated_far).reshape(order, local, width)
    mixed = jnp.einsum("bij,jbd->ibd", lefts, arrived, preferred_element_type=f32).astype(bf16)
    mixed = mixed.reshape(far, near, local, local, width)
    mixed_parts = [from_partner(mixed[:, k], "seq", k) for k in range(near)]
    upward, arrived, mixed_parts[0] = lax.optimization_barrier((upward, arrived, mixed_parts[0]))
    back_pair = jnp.stack([back_far[0], back_far[half]])
    back_pair, mixed_parts = lax.optimization_barrier((back_pair, mixed_parts))
    back_far[0], back_far[half] = back_pair[0], back_pair[1]
    mixed_near = jnp.zeros((far, near, local, local, width), bf16)
    for k, part in enumerate(mixed_parts):
        mixed_near = lax.dynamic_update_index_in_dim(mixed_near, part, device_near ^ k, 1)
    mixed_sent = list(mixed_near)
    back_rest, mixed_rest = lax.optimization_barrier(([back_far[k] for k in rest], [mixed_sent[k] for k in rest]))
    for k, back_part, mixed_part in zip(rest, back_rest, mixed_rest):
        back_far[k], mixed_sent[k] = back_part, mixed_part
    mixed_far = [from_partner(mixed_sent[k], "seq", k << low) for k in range(far)]
    back_near = [from_partner(jnp.stack([t[k] for t in back_far]), "seq", k) for k in range(near)]

    input_view = inputs[0].reshape(local, far, near, local, width)

    def placed(output, part, k):
        place = device_far ^ k
        residual = lax.dynamic_index_in_dim(input_view, place, 1, keepdims=False).astype(f32)
        block = (residual + part.swapaxes(0, 1).astype(f32)).astype(bf16)
        return lax.dynamic_update_index_in_dim(output, block, place, 1)

    output = jnp.zeros((local, far, near, local, width), bf16)
    output = placed(placed(output, mixed_far[0], 0), mixed_far[half], half)
    output, back_near = lax.optimization_barrier((output, back_near))
    dgated = jnp.stack(back_near, axis=1).transpose(2, 0, 1, 3, 4).reshape(local, order, width).astype(f32)

    grad_left = jnp.einsum("ibd,jbd->bij", upward, arrived, preferred_element_type=f32)
    grad_left = sum_over(grad_left, "dp", 0, dp_levels)
    grad_left = jnp.einsum("ki,aij->akj", swap_full, grad_left, precision=lax.Precision.HIGHEST)
    grad_left = jnp.einsum("aij,jl->ail", grad_left, swap_full, precision=lax.Precision.HIGHEST)

    slope = sig * (1.0 - sig)
    dfirst = (dgated * (sig + first * mid_scale * slope)).astype(bf16)
    mid_part = jnp.sum(dgated * first * first * slope, axis=(0, 1))
    grad_right = jnp.einsum("aid,ajd->aij", dfirst, grid, preferred_element_type=f32)
    grad_right = sum_over(grad_right, "dp", 0, dp_levels)
    grad_right = jnp.einsum("ki,aij->akj", swap_full, grad_right, precision=lax.Precision.HIGHEST)
    normalized_gradient = jnp.einsum(
        "aij,aid->ajd", rights, dfirst, preferred_element_type=f32
    ).reshape(rows, width)
    gain_slice = jnp.sum(normalized_gradient * standardized_input, axis=0)
    centered_gradient = normalized_gradient * gain
    input_gradient = upstream[0].astype(f32) + inverse_norm * (
        centered_gradient
        - standardized_input
        * jnp.mean(centered_gradient * standardized_input, axis=-1, keepdims=True)
    )
    input_gradient = input_gradient.astype(bf16)
    vectors = jnp.stack((gain_slice, mid_part))
    vectors = sum_over(vectors, "dp", 0, dp_levels)
    vectors = sum_over(vectors, "seq", 0, low)
    gain_gradient, grad_mid = sum_over(vectors, "seq", low, levels)
    mixed_rest, input_gradient, gain_gradient, grad_mid = lax.optimization_barrier(
        ([mixed_far[k] for k in rest], input_gradient, gain_gradient, grad_mid)
    )
    for k, part in zip(rest, mixed_rest):
        output = placed(output, part, k)
    return (
        output.reshape(1, rows, width),
        input_gradient.reshape(1, rows, width),
        grad_right,
        grad_left,
        gain_gradient,
        grad_mid,
    )


def solution(mesh):
    in_specs = (
        P("dp", "seq", None),
        P("dp", "seq", None),
        P("seq", None, None),
        P("seq", None, None),
        P(),
        P(),
    )
    out_specs = (
        P("dp", "seq", None),
        P("dp", "seq", None),
        P("seq", None, None),
        P("seq", None, None),
        P(),
        P(),
    )
    return jax.shard_map(body, mesh=mesh, in_specs=in_specs, out_specs=out_specs, check_vma=False)
```

```python
import jax
import jax.numpy as jnp
from jax import lax
from jax.sharding import PartitionSpec as P


def from_partner(block, axis, distance):
    if distance == 0:
        return block
    count = lax.axis_size(axis)
    return lax.ppermute(block, axis, [(i, i ^ distance) for i in range(count)])


def tree_sum(terms):
    while len(terms) > 1:
        terms = [terms[i] + terms[i + 1] for i in range(0, len(terms), 2)]
    return terms[0]


def sum_over(value, axis, low, high):
    return tree_sum([from_partner(value, axis, k << low) for k in range(1 << high - low)])


def body(inputs, upstream, right_blocks, left_blocks, gain, mid_scale):
    count = lax.axis_size("seq")
    levels = count.bit_length() - 1
    low = levels // 2
    near = 1 << low
    far = count // near
    dp_levels = lax.axis_size("dp").bit_length() - 1
    device = lax.axis_index("seq")
    device_near = device & near - 1
    device_far = device >> low
    rows = inputs.shape[1]
    width = inputs.shape[2]
    order = right_blocks.shape[1]
    local = order // count
    f32 = jnp.float32
    bf16 = jnp.bfloat16

    place = lax.broadcasted_iota(jnp.int32, (order, order), 0)
    swap = (place ^ device * local) == lax.broadcasted_iota(jnp.int32, (order, order), 1)
    swap_half = swap.astype(bf16)
    swap_full = swap.astype(f32)
    rights = jnp.einsum("ki,aij->akj", swap_half, right_blocks)
    lefts = jnp.einsum("aij,jl->ail", jnp.einsum("ki,aij->akj", swap_half, left_blocks), swap_half)

    half = far // 2
    early, rest = list(range(1, half)), list(range(half + 1, far))

    up_view = upstream[0].reshape(local, far, near, local, width)
    up_parts = [lax.dynamic_index_in_dim(up_view, device_far ^ k, 1, keepdims=False) for k in range(far)]
    up_far = [from_partner(up_parts[k], "seq", k << low) for k in range(far)]
    inputs, up_far[0] = lax.optimization_barrier((inputs, up_far[0]))
    input_float = inputs[0].astype(f32)
    inverse_norm = lax.rsqrt(jnp.mean(input_float * input_float, axis=-1, keepdims=True) + 1e-06)
    standardized_input = input_float * inverse_norm
    normalized_rows = (standardized_input * gain).astype(bf16)
    grid = normalized_rows.reshape(local, order, width)
    first = jnp.einsum("aij,ajd->aid", rights, grid, preferred_element_type=f32)
    sig = jax.nn.sigmoid(first * mid_scale)
    gated = (first * sig).astype(bf16)

    gated_view = gated.reshape(local, far, near, local, width)
    gated_near = [from_partner(gated_view[:, :, k], "seq", k) for k in range(near)]

    def sent_near(part):
        return [lax.dynamic_index_in_dim(part, device_near ^ k, 1, keepdims=False) for k in range(near)]

    up_early = [sent_near(up_far[k]) for k in early]
    up_early, up_far[half] = lax.optimization_barrier((up_early, up_far[half]))
    up_half = sent_near(up_far[half])
    up_half, gated_near = lax.optimization_barrier((up_half, gated_near))
    gated_sent = [jnp.stack([t[:, k] for t in gated_near]) for k in range(far)]
    up_rest, gated_rest = lax.optimization_barrier(([up_far[k] for k in rest], [gated_sent[k] for k in rest]))
    for k, up_part, gated_part in zip(rest, up_rest, gated_rest):
        up_far[k], gated_sent[k] = up_part, gated_part
    gated_far = [from_partner(gated_sent[k], "seq", k << low) for k in range(far)]
    up_sent = [sent_near(up_far[0])] + up_early + [up_half] + [sent_near(up_far[k]) for k in rest]
    up_near = [from_partner(jnp.stack([t[k] for t in up_sent]), "seq", k) for k in range(near)]

    gated_first = jnp.stack(gated_far[:half])
    gated_first, gated_far[half] = lax.optimization_barrier((gated_first, gated_far[half]))
    gated_first = jnp.concatenate([gated_first, gated_far[half][None]])
    gated_first, up_near = lax.optimization_barrier((gated_first, up_near))
    gated_far[: half + 1] = list(gated_first)
    upward = jnp.stack(up_near, axis=1).reshape(order, local, width)
    returned = jnp.einsum("bij,ibd->jbd", lefts, upward, preferred_element_type=f32).astype(bf16)
    returned = list(returned.reshape(far, near, local, local, width))
    gated_rest, returned_rest = lax.optimization_barrier(
        ([gated_far[k] for k in rest], [returned[k] for k in rest])
    )
    for k, gated_part, returned_part in zip(rest, gated_rest, returned_rest):
        gated_far[k], returned[k] = gated_part, returned_part
    back_far = [from_partner(returned[k], "seq", k << low) for k in range(far)]

    arrived = jnp.stack(gated_far).reshape(order, local, width)
    mixed = jnp.einsum("bij,jbd->ibd", lefts, arrived, preferred_element_type=f32).astype(bf16)
    mixed = mixed.reshape(far, near, local, local, width)
    mixed_parts = [from_partner(mixed[:, k], "seq", k) for k in range(near)]
    upward, arrived, mixed_parts[0] = lax.optimization_barrier((upward, arrived, mixed_parts[0]))
    back_first = jnp.stack(back_far[:half])
    back_first, back_far[half] = lax.optimization_barrier((back_first, back_far[half]))
    back_first = jnp.concatenate([back_first, back_far[half][None]])
    back_first, mixed_parts = lax.optimization_barrier((back_first, mixed_parts))
    back_far[: half + 1] = list(back_first)
    mixed_near = jnp.zeros((far, near, local, local, width), bf16)
    for k, part in enumerate(mixed_parts):
        mixed_near = lax.dynamic_update_index_in_dim(mixed_near, part, device_near ^ k, 1)
    mixed_sent = list(mixed_near)
    back_rest, mixed_rest = lax.optimization_barrier(([back_far[k] for k in rest], [mixed_sent[k] for k in rest]))
    for k, back_part, mixed_part in zip(rest, back_rest, mixed_rest):
        back_far[k], mixed_sent[k] = back_part, mixed_part
    mixed_far = [from_partner(mixed_sent[k], "seq", k << low) for k in range(far)]
    back_near = [from_partner(jnp.stack([t[k] for t in back_far]), "seq", k) for k in range(near)]

    input_view = inputs[0].reshape(local, far, near, local, width)

    def placed(output, part, k):
        place = device_far ^ k
        residual = lax.dynamic_index_in_dim(input_view, place, 1, keepdims=False).astype(f32)
        block = (residual + part.swapaxes(0, 1).astype(f32)).astype(bf16)
        return lax.dynamic_update_index_in_dim(output, block, place, 1)

    output = jnp.zeros((local, far, near, local, width), bf16)
    for k in range(half):
        output = placed(output, mixed_far[k], k)
    output, mixed_far[half] = lax.optimization_barrier((output, mixed_far[half]))
    output = placed(output, mixed_far[half], half)
    output, back_near = lax.optimization_barrier((output, back_near))
    dgated = jnp.stack(back_near, axis=1).transpose(2, 0, 1, 3, 4).reshape(local, order, width).astype(f32)

    grad_left = jnp.einsum("ibd,jbd->bij", upward, arrived, preferred_element_type=f32)
    grad_left = sum_over(grad_left, "dp", 0, dp_levels)
    grad_left = jnp.einsum("ki,aij->akj", swap_full, grad_left, precision=lax.Precision.HIGHEST)
    grad_left = jnp.einsum("aij,jl->ail", grad_left, swap_full, precision=lax.Precision.HIGHEST)

    slope = sig * (1.0 - sig)
    dfirst = (dgated * (sig + first * mid_scale * slope)).astype(bf16)
    mid_part = jnp.sum(dgated * first * first * slope, axis=(0, 1))
    grad_right = jnp.einsum("aid,ajd->aij", dfirst, grid, preferred_element_type=f32)
    grad_right = sum_over(grad_right, "dp", 0, dp_levels)
    grad_right = jnp.einsum("ki,aij->akj", swap_full, grad_right, precision=lax.Precision.HIGHEST)
    normalized_gradient = jnp.einsum(
        "aij,aid->ajd", rights, dfirst, preferred_element_type=f32
    ).reshape(rows, width)
    gain_slice = jnp.sum(normalized_gradient * standardized_input, axis=0)
    centered_gradient = normalized_gradient * gain
    input_gradient = upstream[0].astype(f32) + inverse_norm * (
        centered_gradient
        - standardized_input
        * jnp.mean(centered_gradient * standardized_input, axis=-1, keepdims=True)
    )
    input_gradient = input_gradient.astype(bf16)
    vectors = jnp.stack((gain_slice, mid_part))
    vectors = sum_over(vectors, "dp", 0, dp_levels)
    vectors = sum_over(vectors, "seq", 0, low)
    gain_gradient, grad_mid = sum_over(vectors, "seq", low, levels)
    mixed_rest, input_gradient, grad_right, gain_gradient, grad_mid = lax.optimization_barrier(
        ([mixed_far[k] for k in rest], input_gradient, grad_right, gain_gradient, grad_mid)
    )
    for k, part in zip(rest, mixed_rest):
        output = placed(output, part, k)
    return (
        output.reshape(1, rows, width),
        input_gradient.reshape(1, rows, width),
        grad_right,
        grad_left,
        gain_gradient,
        grad_mid,
    )


def solution(mesh):
    in_specs = (
        P("dp", "seq", None),
        P("dp", "seq", None),
        P("seq", None, None),
        P("seq", None, None),
        P(),
        P(),
    )
    out_specs = (
        P("dp", "seq", None),
        P("dp", "seq", None),
        P("seq", None, None),
        P("seq", None, None),
        P(),
        P(),
    )
    return jax.shard_map(body, mesh=mesh, in_specs=in_specs, out_specs=out_specs, check_vma=False)
```

```python
import jax
import jax.numpy as jnp
from jax import lax
from jax.sharding import PartitionSpec as P


def from_partner(block, axis, distance):
    if distance == 0:
        return block
    count = lax.axis_size(axis)
    return lax.ppermute(block, axis, [(i, i ^ distance) for i in range(count)])


def tree_sum(terms):
    while len(terms) > 1:
        terms = [terms[i] + terms[i + 1] for i in range(0, len(terms), 2)]
    return terms[0]


def sum_over(value, axis, low, high):
    return tree_sum([from_partner(value, axis, k << low) for k in range(1 << high - low)])


def body(inputs, upstream, right_blocks, left_blocks, gain, mid_scale):
    count = lax.axis_size("seq")
    levels = count.bit_length() - 1
    low = levels // 2
    near = 1 << low
    far = count // near
    dp_levels = lax.axis_size("dp").bit_length() - 1
    device = lax.axis_index("seq")
    device_near = device & near - 1
    device_far = device >> low
    rows = inputs.shape[1]
    width = inputs.shape[2]
    order = right_blocks.shape[1]
    local = order // count
    f32 = jnp.float32
    bf16 = jnp.bfloat16

    place = lax.broadcasted_iota(jnp.int32, (order, order), 0)
    swap = (place ^ device * local) == lax.broadcasted_iota(jnp.int32, (order, order), 1)
    swap_half = swap.astype(bf16)
    swap_full = swap.astype(f32)
    rights = jnp.einsum("ki,aij->akj", swap_half, right_blocks)
    lefts = jnp.einsum("aij,jl->ail", jnp.einsum("ki,aij->akj", swap_half, left_blocks), swap_half)

    half = far // 2
    rest = [k for k in range(1, far) if k != half]

    up_view = upstream[0].reshape(local, far, near, local, width)
    up_first = lax.dynamic_index_in_dim(up_view, device_far ^ half, 1, keepdims=False)
    up_view, up_first = lax.optimization_barrier((up_view, up_first))
    up_parts = [
        up_first if k == half else lax.dynamic_index_in_dim(up_view, device_far ^ k, 1, keepdims=False)
        for k in range(far)
    ]
    up_far = [from_partner(up_parts[k], "seq", k << low) for k in range(far)]
    inputs, up_far[0] = lax.optimization_barrier((inputs, up_far[0]))
    input_float = inputs[0].astype(f32)
    inverse_norm = lax.rsqrt(jnp.mean(input_float * input_float, axis=-1, keepdims=True) + 1e-06)
    standardized_input = input_float * inverse_norm
    normalized_rows = (standardized_input * gain).astype(bf16)
    grid = normalized_rows.reshape(local, order, width)
    first = jnp.einsum("aij,ajd->aid", rights, grid, preferred_element_type=f32)
    sig = jax.nn.sigmoid(first * mid_scale)
    gated = (first * sig).astype(bf16)

    gated_view = gated.reshape(local, far, near, local, width)
    gated_near = [from_partner(gated_view[:, :, k], "seq", k) for k in range(near)]

    def sent_near(part):
        return [lax.dynamic_index_in_dim(part, device_near ^ k, 1, keepdims=False) for k in range(near)]

    up_half = sent_near(up_far[half])
    up_half, gated_near = lax.optimization_barrier((up_half, gated_near))
    gated_sent = [jnp.stack([t[:, k] for t in gated_near]) for k in range(far)]
    up_rest, gated_rest = lax.optimization_barrier(([up_far[k] for k in rest], [gated_sent[k] for k in rest]))
    for k, up_part, gated_part in zip(rest, up_rest, gated_rest):
        up_far[k], gated_sent[k] = up_part, gated_part
    gated_far = [from_partner(gated_sent[k], "seq", k << low) for k in range(far)]
    up_sent = [up_half if k == half else sent_near(up_far[k]) for k in range(far)]
    up_near = [from_partner(jnp.stack([t[k] for t in up_sent]), "seq", k) for k in range(near)]

    gated_pair = jnp.stack([gated_far[0], gated_far[half]])
    gated_pair, up_near = lax.optimization_barrier((gated_pair, up_near))
    gated_far[0], gated_far[half] = gated_pair[0], gated_pair[1]
    upward = jnp.stack(up_near, axis=1).reshape(order, local, width)
    returned = jnp.einsum("bij,ibd->jbd", lefts, upward, preferred_element_type=f32).astype(bf16)
    returned = list(returned.reshape(far, near, local, local, width))
    gated_rest, returned_rest = lax.optimization_barrier(
        ([gated_far[k] for k in rest], [returned[k] for k in rest])
    )
    for k, gated_part, returned_part in zip(rest, gated_rest, returned_rest):
        gated_far[k], returned[k] = gated_part, returned_part
    back_far = [from_partner(returned[k], "seq", k << low) for k in range(far)]

    arrived = jnp.stack(gated_far).reshape(order, local, width)
    mixed = jnp.einsum("bij,jbd->ibd", lefts, arrived, preferred_element_type=f32).astype(bf16)
    mixed = mixed.reshape(far, near, local, local, width)
    mixed_parts = [from_partner(mixed[:, k], "seq", k) for k in range(near)]
    back_pair = jnp.stack([back_far[0], back_far[half]])
    upward, arrived, back_pair = lax.optimization_barrier((upward, arrived, back_pair))
    grad_left = jnp.einsum("ibd,jbd->bij", upward, arrived, preferred_element_type=f32)
    grad_left, mixed_parts = lax.optimization_barrier((grad_left, mixed_parts))
    grad_left = sum_over(grad_left, "dp", 0, dp_levels)
    grad_left = jnp.einsum("ki,aij->akj", swap_full, grad_left, precision=lax.Precision.HIGHEST)
    grad_left = jnp.einsum("aij,jl->ail", grad_left, swap_full, precision=lax.Precision.HIGHEST)
    back_far[0], back_far[half] = back_pair[0], back_pair[1]
    mixed_near = jnp.zeros((far, near, local, local, width), bf16)
    for k, part in enumerate(mixed_parts):
        mixed_near = lax.dynamic_update_index_in_dim(mixed_near, part, device_near ^ k, 1)
    mixed_sent = list(mixed_near)
    back_rest, mixed_rest = lax.optimization_barrier(([back_far[k] for k in rest], [mixed_sent[k] for k in rest]))
    for k, back_part, mixed_part in zip(rest, back_rest, mixed_rest):
        back_far[k], mixed_sent[k] = back_part, mixed_part
    mixed_far = [from_partner(mixed_sent[k], "seq", k << low) for k in range(far)]
    back_near = [from_partner(jnp.stack([t[k] for t in back_far]), "seq", k) for k in range(near)]

    input_view = inputs[0].reshape(local, far, near, local, width)

    def placed(output, part, k):
        place = device_far ^ k
        residual = lax.dynamic_index_in_dim(input_view, place, 1, keepdims=False).astype(f32)
        block = (residual + part.swapaxes(0, 1).astype(f32)).astype(bf16)
        return lax.dynamic_update_index_in_dim(output, block, place, 1)

    output = jnp.zeros((local, far, near, local, width), bf16)
    output = placed(placed(output, mixed_far[0], 0), mixed_far[half], half)
    output, back_near = lax.optimization_barrier((output, back_near))
    dgated = jnp.stack(back_near, axis=1).transpose(2, 0, 1, 3, 4).reshape(local, order, width).astype(f32)

    slope = sig * (1.0 - sig)
    dfirst = (dgated * (sig + first * mid_scale * slope)).astype(bf16)
    mid_part = jnp.sum(dgated * first * first * slope, axis=(0, 1))
    grad_right = jnp.einsum("aid,ajd->aij", dfirst, grid, preferred_element_type=f32)
    grad_right = sum_over(grad_right, "dp", 0, dp_levels)
    grad_right = jnp.einsum("ki,aij->akj", swap_full, grad_right, precision=lax.Precision.HIGHEST)
    normalized_gradient = jnp.einsum(
        "aij,aid->ajd", rights, dfirst, preferred_element_type=f32
    ).reshape(rows, width)
    gain_slice = jnp.sum(normalized_gradient * standardized_input, axis=0)
    centered_gradient = normalized_gradient * gain
    input_gradient = upstream[0].astype(f32) + inverse_norm * (
        centered_gradient
        - standardized_input
        * jnp.mean(centered_gradient * standardized_input, axis=-1, keepdims=True)
    )
    input_gradient = input_gradient.astype(bf16)
    vectors = jnp.stack((gain_slice, mid_part))
    vectors = sum_over(vectors, "dp", 0, dp_levels)
    vectors = sum_over(vectors, "seq", 0, low)
    gain_gradient, grad_mid = sum_over(vectors, "seq", low, levels)
    mixed_rest, input_gradient, grad_right, gain_gradient, grad_mid = lax.optimization_barrier(
        ([mixed_far[k] for k in rest], input_gradient, grad_right, gain_gradient, grad_mid)
    )
    for k, part in zip(rest, mixed_rest):
        output = placed(output, part, k)
    return (
        output.reshape(1, rows, width),
        input_gradient.reshape(1, rows, width),
        grad_right,
        grad_left,
        gain_gradient,
        grad_mid,
    )


def solution(mesh):
    in_specs = (
        P("dp", "seq", None),
        P("dp", "seq", None),
        P("seq", None, None),
        P("seq", None, None),
        P(),
        P(),
    )
    out_specs = (
        P("dp", "seq", None),
        P("dp", "seq", None),
        P("seq", None, None),
        P("seq", None, None),
        P(),
        P(),
    )
    return jax.shard_map(body, mesh=mesh, in_specs=in_specs, out_specs=out_specs, check_vma=False)
```

```python
import jax
import jax.numpy as jnp
from jax import lax
from jax.sharding import PartitionSpec as P


def from_partner(block, axis, distance):
    if distance == 0:
        return block
    count = lax.axis_size(axis)
    return lax.ppermute(block, axis, [(i, i ^ distance) for i in range(count)])


def tree_sum(terms):
    while len(terms) > 1:
        terms = [terms[i] + terms[i + 1] for i in range(0, len(terms), 2)]
    return terms[0]


def sum_over(value, axis, low, high):
    return tree_sum([from_partner(value, axis, k << low) for k in range(1 << high - low)])


def body(inputs, upstream, right_blocks, left_blocks, gain, mid_scale):
    count = lax.axis_size("seq")
    levels = count.bit_length() - 1
    low = levels // 2
    near = 1 << low
    far = count // near
    dp_levels = lax.axis_size("dp").bit_length() - 1
    device = lax.axis_index("seq")
    device_near = device & near - 1
    device_far = device >> low
    rows = inputs.shape[1]
    width = inputs.shape[2]
    order = right_blocks.shape[1]
    local = order // count
    f32 = jnp.float32
    bf16 = jnp.bfloat16

    place = lax.broadcasted_iota(jnp.int32, (order, order), 0)
    swap = (place ^ device * local) == lax.broadcasted_iota(jnp.int32, (order, order), 1)
    swap_half = swap.astype(bf16)
    swap_full = swap.astype(f32)
    rights = jnp.einsum("ki,aij->akj", swap_half, right_blocks)
    lefts = jnp.einsum("aij,jl->ail", jnp.einsum("ki,aij->akj", swap_half, left_blocks), swap_half)

    half = far // 2
    rest = [k for k in range(1, far) if k != half]

    up_view = upstream[0].reshape(local, far, near, local, width)
    up_first = lax.dynamic_index_in_dim(up_view, device_far ^ half, 1, keepdims=False)
    up_view, up_first = lax.optimization_barrier((up_view, up_first))
    up_parts = [
        up_first if k == half else lax.dynamic_index_in_dim(up_view, device_far ^ k, 1, keepdims=False)
        for k in range(far)
    ]
    up_far = [from_partner(up_parts[k], "seq", k << low) for k in range(far)]
    inputs, up_far[0] = lax.optimization_barrier((inputs, up_far[0]))
    input_float = inputs[0].astype(f32)
    inverse_norm = lax.rsqrt(jnp.mean(input_float * input_float, axis=-1, keepdims=True) + 1e-06)
    standardized_input = input_float * inverse_norm
    normalized_rows = (standardized_input * gain).astype(bf16)
    grid = normalized_rows.reshape(local, order, width)
    first = jnp.einsum("aij,ajd->aid", rights, grid, preferred_element_type=f32)
    sig = jax.nn.sigmoid(first * mid_scale)
    gated = (first * sig).astype(bf16)

    gated_view = gated.reshape(local, far, near, local, width)
    gated_near = [from_partner(gated_view[:, :, k], "seq", k) for k in range(near)]

    def sent_near(part):
        return [lax.dynamic_index_in_dim(part, device_near ^ k, 1, keepdims=False) for k in range(near)]

    up_half = sent_near(up_far[half])
    up_half, gated_near = lax.optimization_barrier((up_half, gated_near))
    gated_sent = [jnp.stack([t[:, k] for t in gated_near]) for k in range(far)]
    up_rest, gated_rest = lax.optimization_barrier(([up_far[k] for k in rest], [gated_sent[k] for k in rest]))
    for k, up_part, gated_part in zip(rest, up_rest, gated_rest):
        up_far[k], gated_sent[k] = up_part, gated_part
    gated_far = [from_partner(gated_sent[k], "seq", k << low) for k in range(far)]
    up_sent = [up_half if k == half else sent_near(up_far[k]) for k in range(far)]
    up_near = [from_partner(jnp.stack([t[k] for t in up_sent]), "seq", k) for k in range(near)]

    gated_pair = jnp.stack([gated_far[0], gated_far[half]])
    gated_pair, up_near = lax.optimization_barrier((gated_pair, up_near))
    gated_far[0], gated_far[half] = gated_pair[0], gated_pair[1]
    upward = jnp.stack(up_near, axis=1).reshape(order, local, width)
    returned = jnp.einsum("bij,ibd->jbd", lefts, upward, preferred_element_type=f32).astype(bf16)
    returned = list(returned.reshape(far, near, local, local, width))
    gated_rest, returned_rest = lax.optimization_barrier(
        ([gated_far[k] for k in rest], [returned[k] for k in rest])
    )
    for k, gated_part, returned_part in zip(rest, gated_rest, returned_rest):
        gated_far[k], returned[k] = gated_part, returned_part
    back_far = [from_partner(returned[k], "seq", k << low) for k in range(far)]

    arrived = jnp.stack(gated_far).reshape(order, local, width)
    mixed = jnp.einsum("bij,jbd->ibd", lefts, arrived, preferred_element_type=f32).astype(bf16)
    mixed = mixed.reshape(far, near, local, local, width)
    mixed_parts = [from_partner(mixed[:, k], "seq", k) for k in range(near)]
    back_pair = jnp.stack([back_far[0], back_far[half]])
    upward, arrived, back_pair = lax.optimization_barrier((upward, arrived, back_pair))
    grad_left = jnp.einsum("ibd,jbd->bij", upward, arrived, preferred_element_type=f32)
    grad_left = sum_over(grad_left, "dp", 0, dp_levels)
    grad_left = jnp.einsum("ki,aij->akj", swap_full, grad_left, precision=lax.Precision.HIGHEST)
    grad_left = jnp.einsum("aij,jl->ail", grad_left, swap_full, precision=lax.Precision.HIGHEST)
    grad_left, mixed_parts = lax.optimization_barrier((grad_left, mixed_parts))
    back_far[0], back_far[half] = back_pair[0], back_pair[1]
    mixed_near = jnp.zeros((far, near, local, local, width), bf16)
    for k, part in enumerate(mixed_parts):
        mixed_near = lax.dynamic_update_index_in_dim(mixed_near, part, device_near ^ k, 1)
    mixed_sent = list(mixed_near)
    back_rest, mixed_rest = lax.optimization_barrier(([back_far[k] for k in rest[::-1]], [mixed_sent[k] for k in rest[::-1]]))
    for k, back_part, mixed_part in zip(rest[::-1], back_rest, mixed_rest):
        back_far[k], mixed_sent[k] = back_part, mixed_part
    mixed_far = [from_partner(mixed_sent[k], "seq", k << low) for k in range(far)]
    back_near = [from_partner(jnp.stack([t[k] for t in back_far]), "seq", k) for k in range(near)]

    input_view = inputs[0].reshape(local, far, near, local, width)

    def placed(output, part, k):
        place = device_far ^ k
        residual = lax.dynamic_index_in_dim(input_view, place, 1, keepdims=False).astype(f32)
        block = (residual + part.swapaxes(0, 1).astype(f32)).astype(bf16)
        return lax.dynamic_update_index_in_dim(output, block, place, 1)

    output = jnp.zeros((local, far, near, local, width), bf16)
    output = placed(placed(output, mixed_far[0], 0), mixed_far[half], half)
    output, back_near = lax.optimization_barrier((output, back_near))
    dgated = jnp.stack(back_near, axis=1).transpose(2, 0, 1, 3, 4).reshape(local, order, width).astype(f32)

    slope = sig * (1.0 - sig)
    dfirst = (dgated * (sig + first * mid_scale * slope)).astype(bf16)
    mid_part = jnp.sum(dgated * first * first * slope, axis=(0, 1))
    grad_right = jnp.einsum("aid,ajd->aij", dfirst, grid, preferred_element_type=f32)
    grad_right = sum_over(grad_right, "dp", 0, dp_levels)
    grad_right = jnp.einsum("ki,aij->akj", swap_full, grad_right, precision=lax.Precision.HIGHEST)
    normalized_gradient = jnp.einsum(
        "aij,aid->ajd", rights, dfirst, preferred_element_type=f32
    ).reshape(rows, width)
    gain_slice = jnp.sum(normalized_gradient * standardized_input, axis=0)
    centered_gradient = normalized_gradient * gain
    input_gradient = upstream[0].astype(f32) + inverse_norm * (
        centered_gradient
        - standardized_input
        * jnp.mean(centered_gradient * standardized_input, axis=-1, keepdims=True)
    )
    input_gradient = input_gradient.astype(bf16)
    vectors = jnp.stack((gain_slice, mid_part))
    vectors = sum_over(vectors, "dp", 0, dp_levels)
    vectors = sum_over(vectors, "seq", 0, low)
    gain_gradient, grad_mid = sum_over(vectors, "seq", low, levels)
    mixed_rest, input_gradient, grad_right, gain_gradient, grad_mid = lax.optimization_barrier(
        ([mixed_far[k] for k in rest], input_gradient, grad_right, gain_gradient, grad_mid)
    )
    for k, part in zip(rest, mixed_rest):
        output = placed(output, part, k)
    return (
        output.reshape(1, rows, width),
        input_gradient.reshape(1, rows, width),
        grad_right,
        grad_left,
        gain_gradient,
        grad_mid,
    )


def solution(mesh):
    in_specs = (
        P("dp", "seq", None),
        P("dp", "seq", None),
        P("seq", None, None),
        P("seq", None, None),
        P(),
        P(),
    )
    out_specs = (
        P("dp", "seq", None),
        P("dp", "seq", None),
        P("seq", None, None),
        P("seq", None, None),
        P(),
        P(),
    )
    return jax.shard_map(body, mesh=mesh, in_specs=in_specs, out_specs=out_specs, check_vma=False)
```

```python
import jax
import jax.numpy as jnp
from jax import lax
from jax.sharding import PartitionSpec as P


def from_partner(block, axis, distance):
    if distance == 0:
        return block
    count = lax.axis_size(axis)
    return lax.ppermute(block, axis, [(i, i ^ distance) for i in range(count)])


def tree_sum(terms):
    while len(terms) > 1:
        terms = [terms[i] + terms[i + 1] for i in range(0, len(terms), 2)]
    return terms[0]


def sum_over(value, axis, low, high):
    return tree_sum([from_partner(value, axis, k << low) for k in range(1 << high - low)])


def body(inputs, upstream, right_blocks, left_blocks, gain, mid_scale):
    count = lax.axis_size("seq")
    levels = count.bit_length() - 1
    low = levels // 2
    near = 1 << low
    far = count // near
    dp_levels = lax.axis_size("dp").bit_length() - 1
    device = lax.axis_index("seq")
    device_near = device & near - 1
    device_far = device >> low
    rows = inputs.shape[1]
    width = inputs.shape[2]
    order = right_blocks.shape[1]
    local = order // count
    f32 = jnp.float32
    bf16 = jnp.bfloat16

    place = lax.broadcasted_iota(jnp.int32, (order, order), 0)
    swap = (place ^ device * local) == lax.broadcasted_iota(jnp.int32, (order, order), 1)
    swap_half = swap.astype(bf16)
    swap_full = swap.astype(f32)
    rights = jnp.einsum("ki,aij->akj", swap_half, right_blocks)
    lefts = jnp.einsum("aij,jl->ail", jnp.einsum("ki,aij->akj", swap_half, left_blocks), swap_half)

    half = far // 2
    rest = [k for k in range(1, far) if k != half]

    up_view = upstream[0].reshape(local, far, near, local, width)
    up_first = lax.dynamic_index_in_dim(up_view, device_far ^ half, 1, keepdims=False)
    up_view, up_first = lax.optimization_barrier((up_view, up_first))
    up_parts = [
        up_first if k == half else lax.dynamic_index_in_dim(up_view, device_far ^ k, 1, keepdims=False)
        for k in range(far)
    ]
    up_far = [from_partner(up_parts[k], "seq", k << low) for k in range(far)]
    inputs, up_far[0] = lax.optimization_barrier((inputs, up_far[0]))
    input_float = inputs[0].astype(f32)
    inverse_norm = lax.rsqrt(jnp.mean(input_float * input_float, axis=-1, keepdims=True) + 1e-06)
    standardized_input = input_float * inverse_norm
    normalized_rows = (standardized_input * gain).astype(bf16)
    grid = normalized_rows.reshape(local, order, width)
    first = jnp.einsum("aij,ajd->aid", rights, grid, preferred_element_type=f32)
    sig = jax.nn.sigmoid(first * mid_scale)
    gated = (first * sig).astype(bf16)

    gated_view = gated.reshape(local, far, near, local, width)
    gated_near = [from_partner(gated_view[:, :, k], "seq", k) for k in range(near)]

    def sent_near(part):
        return [lax.dynamic_index_in_dim(part, device_near ^ k, 1, keepdims=False) for k in range(near)]

    up_half = sent_near(up_far[half])
    up_half, gated_near = lax.optimization_barrier((up_half, gated_near))
    gated_sent = [jnp.stack([t[:, k] for t in gated_near]) for k in range(far)]
    up_rest, gated_sent = lax.optimization_barrier(([up_far[k] for k in rest], gated_sent))
    for k, up_part in zip(rest, up_rest):
        up_far[k] = up_part
    gated_far = [from_partner(gated_sent[k], "seq", k << low) for k in range(far)]
    up_sent = [up_half if k == half else sent_near(up_far[k]) for k in range(far)]
    up_near = [from_partner(jnp.stack([t[k] for t in up_sent]), "seq", k) for k in range(near)]

    gated_pair = jnp.stack([gated_far[0], gated_far[half]])
    gated_pair, up_near = lax.optimization_barrier((gated_pair, up_near))
    gated_far[0], gated_far[half] = gated_pair[0], gated_pair[1]
    upward = jnp.stack(up_near, axis=1).reshape(order, local, width)
    returned = jnp.einsum("bij,ibd->jbd", lefts, upward, preferred_element_type=f32).astype(bf16)
    returned = list(returned.reshape(far, near, local, local, width))
    gated_rest, returned_rest = lax.optimization_barrier(
        ([gated_far[k] for k in rest], [returned[k] for k in rest])
    )
    for k, gated_part, returned_part in zip(rest, gated_rest, returned_rest):
        gated_far[k], returned[k] = gated_part, returned_part
    back_far = [from_partner(returned[k], "seq", k << low) for k in range(far)]

    arrived = jnp.stack(gated_far).reshape(order, local, width)
    mixed = jnp.einsum("bij,jbd->ibd", lefts, arrived, preferred_element_type=f32).astype(bf16)
    mixed = mixed.reshape(far, near, local, local, width)
    mixed_parts = [from_partner(mixed[:, k], "seq", k) for k in range(near)]
    upward, arrived, mixed_parts[0] = lax.optimization_barrier((upward, arrived, mixed_parts[0]))
    back_pair = jnp.stack([back_far[0], back_far[half]])
    back_pair, mixed_parts = lax.optimization_barrier((back_pair, mixed_parts))
    back_far[0], back_far[half] = back_pair[0], back_pair[1]
    mixed_near = jnp.zeros((far, near, local, local, width), bf16)
    for k, part in enumerate(mixed_parts):
        mixed_near = lax.dynamic_update_index_in_dim(mixed_near, part, device_near ^ k, 1)
    mixed_sent = list(mixed_near)
    back_rest, mixed_rest = lax.optimization_barrier(([back_far[k] for k in rest], [mixed_sent[k] for k in rest]))
    for k, back_part, mixed_part in zip(rest, back_rest, mixed_rest):
        back_far[k], mixed_sent[k] = back_part, mixed_part
    mixed_far = [from_partner(mixed_sent[k], "seq", k << low) for k in range(far)]
    back_near = [from_partner(jnp.stack([t[k] for t in back_far]), "seq", k) for k in range(near)]

    input_view = inputs[0].reshape(local, far, near, local, width)

    def placed(output, part, k):
        place = device_far ^ k
        residual = lax.dynamic_index_in_dim(input_view, place, 1, keepdims=False).astype(f32)
        block = (residual + part.swapaxes(0, 1).astype(f32)).astype(bf16)
        return lax.dynamic_update_index_in_dim(output, block, place, 1)

    output = jnp.zeros((local, far, near, local, width), bf16)
    output = placed(placed(output, mixed_far[0], 0), mixed_far[half], half)
    output, back_near = lax.optimization_barrier((output, back_near))
    dgated = jnp.stack(back_near, axis=1).transpose(2, 0, 1, 3, 4).reshape(local, order, width).astype(f32)

    grad_left = jnp.einsum("ibd,jbd->bij", upward, arrived, preferred_element_type=f32)
    grad_left = sum_over(grad_left, "dp", 0, dp_levels)
    grad_left = jnp.einsum("ki,aij->akj", swap_full, grad_left, precision=lax.Precision.HIGHEST)
    grad_left = jnp.einsum("aij,jl->ail", grad_left, swap_full, precision=lax.Precision.HIGHEST)

    slope = sig * (1.0 - sig)
    dfirst = (dgated * (sig + first * mid_scale * slope)).astype(bf16)
    mid_part = jnp.sum(dgated * first * first * slope, axis=(0, 1))
    grad_right = jnp.einsum("aid,ajd->aij", dfirst, grid, preferred_element_type=f32)
    grad_right = sum_over(grad_right, "dp", 0, dp_levels)
    grad_right = jnp.einsum("ki,aij->akj", swap_full, grad_right, precision=lax.Precision.HIGHEST)
    normalized_gradient = jnp.einsum(
        "aij,aid->ajd", rights, dfirst, preferred_element_type=f32
    ).reshape(rows, width)
    gain_slice = jnp.sum(normalized_gradient * standardized_input, axis=0)
    centered_gradient = normalized_gradient * gain
    input_gradient = upstream[0].astype(f32) + inverse_norm * (
        centered_gradient
        - standardized_input
        * jnp.mean(centered_gradient * standardized_input, axis=-1, keepdims=True)
    )
    input_gradient = input_gradient.astype(bf16)
    vectors = jnp.stack((gain_slice, mid_part))
    vectors = sum_over(vectors, "dp", 0, dp_levels)
    vectors = sum_over(vectors, "seq", 0, low)
    gain_gradient, grad_mid = sum_over(vectors, "seq", low, levels)
    mixed_rest, input_gradient, gain_gradient, grad_mid = lax.optimization_barrier(
        ([mixed_far[k] for k in rest], input_gradient, gain_gradient, grad_mid)
    )
    for k, part in zip(rest, mixed_rest):
        output = placed(output, part, k)
    return (
        output.reshape(1, rows, width),
        input_gradient.reshape(1, rows, width),
        grad_right,
        grad_left,
        gain_gradient,
        grad_mid,
    )


def solution(mesh):
    in_specs = (
        P("dp", "seq", None),
        P("dp", "seq", None),
        P("seq", None, None),
        P("seq", None, None),
        P(),
        P(),
    )
    out_specs = (
        P("dp", "seq", None),
        P("dp", "seq", None),
        P("seq", None, None),
        P("seq", None, None),
        P(),
        P(),
    )
    return jax.shard_map(body, mesh=mesh, in_specs=in_specs, out_specs=out_specs, check_vma=False)
```

```python
import jax
import jax.numpy as jnp
from jax import lax
from jax.sharding import PartitionSpec as P


def from_partner(block, axis, distance):
    if distance == 0:
        return block
    count = lax.axis_size(axis)
    return lax.ppermute(block, axis, [(i, i ^ distance) for i in range(count)])


def tree_sum(terms):
    while len(terms) > 1:
        terms = [terms[i] + terms[i + 1] for i in range(0, len(terms), 2)]
    return terms[0]


def sum_over(value, axis, low, high):
    return tree_sum([from_partner(value, axis, k << low) for k in range(1 << high - low)])


def body(inputs, upstream, right_blocks, left_blocks, gain, mid_scale):
    count = lax.axis_size("seq")
    levels = count.bit_length() - 1
    low = levels // 2
    near = 1 << low
    far = count // near
    dp_levels = lax.axis_size("dp").bit_length() - 1
    device = lax.axis_index("seq")
    device_near = device & near - 1
    device_far = device >> low
    rows = inputs.shape[1]
    width = inputs.shape[2]
    order = right_blocks.shape[1]
    local = order // count
    f32 = jnp.float32
    bf16 = jnp.bfloat16

    place = lax.broadcasted_iota(jnp.int32, (order, order), 0)
    swap = (place ^ device * local) == lax.broadcasted_iota(jnp.int32, (order, order), 1)
    swap_half = swap.astype(bf16)
    swap_full = swap.astype(f32)
    rights = jnp.einsum("ki,aij->akj", swap_half, right_blocks)
    lefts = jnp.einsum("aij,jl->ail", jnp.einsum("ki,aij->akj", swap_half, left_blocks), swap_half)

    half = far // 2
    rest = [k for k in range(1, far) if k != half]

    up_view = upstream[0].reshape(local, far, near, local, width)
    up_first = lax.dynamic_index_in_dim(up_view, device_far ^ half, 1, keepdims=False)
    up_view, up_first = lax.optimization_barrier((up_view, up_first))
    up_parts = [
        up_first if k == half else lax.dynamic_index_in_dim(up_view, device_far ^ k, 1, keepdims=False)
        for k in range(far)
    ]
    up_far = [from_partner(up_parts[k], "seq", k << low) for k in range(far)]
    inputs, up_far[0] = lax.optimization_barrier((inputs, up_far[0]))
    input_float = inputs[0].astype(f32)
    inverse_norm = lax.rsqrt(jnp.mean(input_float * input_float, axis=-1, keepdims=True) + 1e-06)
    standardized_input = input_float * inverse_norm
    normalized_rows = (standardized_input * gain).astype(bf16)
    grid = normalized_rows.reshape(local, order, width)
    first = jnp.einsum("aij,ajd->aid", rights, grid, preferred_element_type=f32)
    sig = jax.nn.sigmoid(first * mid_scale)
    gated = (first * sig).astype(bf16)

    gated_view = gated.reshape(local, far, near, local, width)
    gated_near = [from_partner(gated_view[:, :, k], "seq", k) for k in range(near)]

    def sent_near(part):
        return [lax.dynamic_index_in_dim(part, device_near ^ k, 1, keepdims=False) for k in range(near)]

    up_half = sent_near(up_far[half])
    up_half, gated_near = lax.optimization_barrier((up_half, gated_near))
    gated_sent = [jnp.stack([t[:, k] for t in gated_near]) for k in range(far)]
    up_rest, gated_sent = lax.optimization_barrier(([up_far[k] for k in rest], gated_sent))
    for k, up_part in zip(rest, up_rest):
        up_far[k] = up_part
    gated_far = [from_partner(gated_sent[k], "seq", k << low) for k in range(far)]
    up_sent = [up_half if k == half else sent_near(up_far[k]) for k in range(far)]
    up_near = [from_partner(jnp.stack([t[k] for t in up_sent]), "seq", k) for k in range(near)]

    gated_pair = jnp.stack([gated_far[0], gated_far[half]])
    gated_pair, up_near = lax.optimization_barrier((gated_pair, up_near))
    gated_far[0], gated_far[half] = gated_pair[0], gated_pair[1]
    upward = jnp.stack(up_near, axis=1).reshape(order, local, width)
    returned = jnp.einsum("bij,ibd->jbd", lefts, upward, preferred_element_type=f32).astype(bf16)
    returned = list(returned.reshape(far, near, local, local, width))
    gated_rest, returned_rest = lax.optimization_barrier(
        ([gated_far[k] for k in rest], [returned[k] for k in rest])
    )
    for k, gated_part, returned_part in zip(rest, gated_rest, returned_rest):
        gated_far[k], returned[k] = gated_part, returned_part
    back_far = [from_partner(returned[k], "seq", k << low) for k in range(far)]

    arrived = jnp.stack(gated_far).reshape(order, local, width)
    mixed = jnp.einsum("bij,jbd->ibd", lefts, arrived, preferred_element_type=f32).astype(bf16)
    mixed = mixed.reshape(far, near, local, local, width)
    mixed_parts = [from_partner(mixed[:, k], "seq", k) for k in range(near)]
    upward, arrived, mixed_parts[0] = lax.optimization_barrier((upward, arrived, mixed_parts[0]))
    back_pair = jnp.stack([back_far[0], back_far[half]])
    back_pair, mixed_parts = lax.optimization_barrier((back_pair, mixed_parts))
    back_far[0], back_far[half] = back_pair[0], back_pair[1]
    mixed_near = jnp.zeros((far, near, local, local, width), bf16)
    for k, part in enumerate(mixed_parts):
        mixed_near = lax.dynamic_update_index_in_dim(mixed_near, part, device_near ^ k, 1)
    mixed_sent = list(mixed_near)
    back_rest, mixed_rest = lax.optimization_barrier(([back_far[k] for k in rest], [mixed_sent[k] for k in rest]))
    for k, back_part, mixed_part in zip(rest, back_rest, mixed_rest):
        back_far[k], mixed_sent[k] = back_part, mixed_part
    mixed_far = [from_partner(mixed_sent[k], "seq", k << low) for k in range(far)]
    back_near = [from_partner(jnp.stack([t[k] for t in back_far]), "seq", k) for k in range(near)]

    input_view = inputs[0].reshape(local, far, near, local, width)

    def placed(output, part, k):
        place = device_far ^ k
        residual = lax.dynamic_index_in_dim(input_view, place, 1, keepdims=False).astype(f32)
        block = (residual + part.swapaxes(0, 1).astype(f32)).astype(bf16)
        return lax.dynamic_update_index_in_dim(output, block, place, 1)

    output = jnp.zeros((local, far, near, local, width), bf16)
    output = placed(placed(output, mixed_far[0], 0), mixed_far[half], half)
    output, back_near = lax.optimization_barrier((output, back_near))
    dgated = jnp.stack(back_near, axis=1).transpose(2, 0, 1, 3, 4).reshape(local, order, width).astype(f32)

    grad_left = jnp.einsum("ibd,jbd->bij", upward, arrived, preferred_element_type=f32)
    grad_left = sum_over(grad_left, "dp", 0, dp_levels)
    grad_left = jnp.einsum("ki,aij->akj", swap_full, grad_left, precision=lax.Precision.HIGHEST)
    grad_left = jnp.einsum("aij,jl->ail", grad_left, swap_full, precision=lax.Precision.HIGHEST)

    slope = sig * (1.0 - sig)
    dfirst = (dgated * (sig + first * mid_scale * slope)).astype(bf16)
    mid_part = jnp.sum(dgated * first * first * slope, axis=(0, 1))
    grad_right = jnp.einsum("aid,ajd->aij", dfirst, grid, preferred_element_type=f32)
    grad_right = sum_over(grad_right, "dp", 0, dp_levels)
    grad_right = jnp.einsum("ki,aij->akj", swap_full, grad_right, precision=lax.Precision.HIGHEST)
    normalized_gradient = jnp.einsum(
        "aij,aid->ajd", rights, dfirst, preferred_element_type=f32
    ).reshape(rows, width)
    gain_slice = jnp.sum(normalized_gradient * standardized_input, axis=0)
    centered_gradient = normalized_gradient * gain
    input_gradient = upstream[0].astype(f32) + inverse_norm * (
        centered_gradient
        - standardized_input
        * jnp.mean(centered_gradient * standardized_input, axis=-1, keepdims=True)
    )
    input_gradient = input_gradient.astype(bf16)
    vectors = jnp.stack((gain_slice, mid_part))
    vectors = sum_over(vectors, "dp", 0, dp_levels)
    vectors = sum_over(vectors, "seq", 0, low)
    vectors, grad_right = lax.optimization_barrier((vectors, grad_right))
    gain_gradient, grad_mid = sum_over(vectors, "seq", low, levels)
    mixed_rest, input_gradient, gain_gradient, grad_mid = lax.optimization_barrier(
        ([mixed_far[k] for k in rest], input_gradient, gain_gradient, grad_mid)
    )
    for k, part in zip(rest, mixed_rest):
        output = placed(output, part, k)
    return (
        output.reshape(1, rows, width),
        input_gradient.reshape(1, rows, width),
        grad_right,
        grad_left,
        gain_gradient,
        grad_mid,
    )


def solution(mesh):
    in_specs = (
        P("dp", "seq", None),
        P("dp", "seq", None),
        P("seq", None, None),
        P("seq", None, None),
        P(),
        P(),
    )
    out_specs = (
        P("dp", "seq", None),
        P("dp", "seq", None),
        P("seq", None, None),
        P("seq", None, None),
        P(),
        P(),
    )
    return jax.shard_map(body, mesh=mesh, in_specs=in_specs, out_specs=out_specs, check_vma=False)
```
